32 devices in a mesh: group: 2 (over y), expert: 4 (over z), tensor: 4 (over x, core).
Axes of the slice: x: 2, y: 2, z: 4, core: 2. Of those that a mesh axis runs over, the one named last changes fastest.
Arguments:
- tokens: bfloat16 [512, 4096], P(('group', 'expert'), 'tensor'), parts along dimension 0, may hold values from -400 to 400
- norm_gain: float32 [4096], replicated, may hold values from 0.1 to 1.9
- expert_ids: int32 [512, 8], P(('group', 'expert')), parts along dimension 0, may hold values from 0 to 63, all different within a row; in each aligned block of 64 rows (0 to 63, 64 to 127, ...) at most 16 rows name the same one
- gate_weights: float32 [512, 8], P(('group', 'expert')), parts along dimension 0, may hold values from 0.1 to 1
- gate_proj: bfloat16 [64, 768, 4096], P('expert', 'tensor'), may hold values from -0.09375 to 0.09375
- up_proj: bfloat16 [64, 768, 4096], P('expert', 'tensor'), may hold values from -0.09375 to 0.09375
- down_proj: bfloat16 [64, 4096, 768], P('expert', 'tensor'), may hold values from -0.21875 to 0.21875
Outputs:
- moe_out: bfloat16 [512, 4096], P(('group', 'expert'), 'tensor'), parts along dimension 0
The draws below stay inside these ranges and needn't reach their ends.
There are 2 independent parts, one for each index of `group`. The reference program is written for one: setup_inputs(seed, part) draws one part's arguments, and reference() takes and returns one part's arrays. A program takes and returns all parts, laid end to end along the dimension named above; an argument that names none is the same for every part. Nothing has to cross between parts.
Inputs may be any that keep to these rules, and one draw needn't show every extreme that they name: `expert_ids`: each row names 8 different experts. Within the rows of one device (aligned blocks of 64 rows) no expert is named by more than 16 rows, a bound that some block reaches.
All inputs are finite; a program needn't handle non-finite values.
Results may differ from the reference program's by a relative error of at most 0.008.
Values may be sent and summed in bfloat16 or wider, within the bound.
A program may use at most 128 MiB of HBM per device.

```python
import math
import jax
import jax.numpy as jnp
import numpy as np
from jax import lax

D = 4096
FF = 768
EXPERTS = 64
TOP = 8
TOK_DEV = 64
CAP = 16
TOKENS = 256


def draw_tokens(key, part):
    base_key = jax.random.fold_in(key, 7)
    row_key, col_key, draw_key = jax.random.split(base_key, 3)
    row_scale = jnp.exp(jax.random.uniform(row_key, (TOKENS, 1), jnp.float32, 0.0, math.log(10.0)))
    col_scale = jnp.exp(jax.random.uniform(col_key, (1, D), jnp.float32, 0.0, math.log(10.0)))
    base_draw = jnp.clip(jax.random.normal(draw_key, (TOKENS, D), jnp.float32), -4.0, 4.0)
    return (base_draw * row_scale * col_scale).astype(jnp.bfloat16)


def level_of(stream_key, shape, cuts, smallest, largest):
    factor_of = 1.0
    for axis_at, parts in cuts:
        draws = jax.random.uniform(jax.random.fold_in(jax.random.fold_in(stream_key, 6), axis_at), (parts,), jnp.float32, smallest / len(cuts), largest / len(cuts))
        factor_of = factor_of * jnp.repeat(jnp.exp(draws), shape[axis_at] // parts).reshape((-1,) + (1,) * (len(shape) - 1 - axis_at))
    return factor_of


def deal_out(own_key, own, number, rows, count, top, most, slope):
    sequence = jax.random.permutation(own_key, count)
    packed, common = shares(count, rows * top, most, slope, True), shares(count, rows * top, most, slope, False)
    places = jnp.arange(count)

    def named(lengths, rotation):
        used = int((lengths > 0).sum())
        fixed = max(1, used // 4)
        shifted = fixed + (places - fixed + rotation * (used - fixed)) % max(1, count - fixed)
        return jnp.zeros((count,), jnp.int32).at[sequence[jnp.where(places < fixed, places, shifted)]].set(jnp.asarray(lengths, jnp.int32))

    lengths = jnp.where(number % 4 == 0, named(packed, number // 4), named(common, number - number // 4 - 1))
    mixed = jax.random.permutation(jax.random.fold_in(own, 3), count)
    donor, sink = mixed[0:count // 2 * 2:2], mixed[1:count // 2 * 2:2]
    slack = jnp.minimum(lengths[donor] - 1, most - lengths[sink]) // 2
    slack = jnp.where((donor == sequence[0]) | (sink == sequence[0]) | (lengths[sink] == 0), 0, jnp.maximum(slack, 0))
    shifted = jax.random.randint(jax.random.fold_in(own, 4), (count // 2,), 0, 1 << 20) % (slack + 1)
    lengths = lengths.at[donor].add(-shifted).at[sink].add(shifted)
    labels = jnp.searchsorted(jnp.cumsum(lengths), jnp.arange(rows * top), side="right").astype(jnp.int32)
    grid = labels.reshape(top, rows).T
    grid = grid[jax.random.permutation(jax.random.fold_in(own, 1), rows)]
    rotation = jax.random.randint(jax.random.fold_in(own, 2), (rows, 1), 0, top)
    return jnp.take_along_axis(grid, (jnp.arange(top)[None, :] + rotation) % top, axis=1)


def shares(amount, total, reach, slope, full):
    portions = [(1 << 20) // math.isqrt(standing ** slope) + 1 for standing in range(1, amount + 1)]
    largest = reach if full else min(reach, max(-(-total // amount), total * portions[0] // sum(portions)))
    least = 1 if total - largest >= amount - 1 else 0
    holding, surplus = [largest] + [least] * (amount - 1), total - largest - least * (amount - 1)
    while surplus > 0:
        movable = [i for i in range(1, amount) if holding[i] < largest] or [i for i in range(1, amount) if holding[i] < reach]
        pool, left = sum([portions[i] for i in movable]), surplus
        for i in movable:
            extra = min(reach - holding[i], max(1, left * portions[i] // pool), surplus)
            holding[i] = holding[i] + extra
            surplus = surplus - extra
    return np.array(holding)


def scatter_about(rng, dims, scale, most, shards=(), held_as=jnp.bfloat16):
    gain = level_of(rng, dims, shards, -0.22, 0.18) if shards else 1.0
    array = jax.random.normal(rng, dims, jnp.float32) * scale * gain
    return jnp.minimum(jnp.maximum(array, -most), most).astype(held_as)


def setup_inputs(seed: int = 0, part: int = 0) -> dict:
    key_of = jax.random.split(jax.random.key(seed), 8)
    part_splits = jax.random.split(jax.random.fold_in(key_of[7], part), 8)
    tokens = draw_tokens(jax.random.fold_in(jax.random.fold_in(key_of[7], part), 71), part)
    norm_gain = jnp.clip(1.0 + 0.18 * jax.random.normal(key_of[1], (D,), jnp.float32), 0.1, 1.9)
    expert_ids_keys = jax.random.split(jax.random.fold_in(part_splits[2], 1), TOKENS // TOK_DEV)
    expert_ids_turns = jax.random.permutation(jax.random.fold_in(part_splits[2], 3), TOKENS // TOK_DEV)
    expert_ids = jax.vmap(lambda own, number: deal_out(jax.random.fold_in(part_splits[2], 2), own, number, TOK_DEV, EXPERTS, TOP, CAP, 2))(expert_ids_keys, expert_ids_turns).reshape((TOKENS, TOP))
    gate_weights = jnp.clip(0.1 + 0.9 * jax.random.uniform(part_splits[3], (TOKENS, TOP), jnp.float32) ** level_of(part_splits[3], (TOKENS, TOP), ((0, 4),), -0.2, 0.2), 0.1, 1.0)
    gate_proj = scatter_about(key_of[4], (EXPERTS, FF, D), D ** -0.5, 0.09375, ((0, 4), (1, 4)))
    up_proj = scatter_about(key_of[5], (EXPERTS, FF, D), D ** -0.5, 0.09375, ((0, 4), (1, 4)))
    down_proj = scatter_about(key_of[6], (EXPERTS, D, FF), FF ** -0.5, 0.21875, ((0, 4), (1, 4)))
    return dict(tokens=tokens, norm_gain=norm_gain, expert_ids=expert_ids, gate_weights=gate_weights, gate_proj=gate_proj, up_proj=up_proj, down_proj=down_proj)


def reference(tokens, norm_gain, expert_ids, gate_weights, gate_proj, up_proj, down_proj):
    values = tokens.astype(jnp.float32)
    inv_scale = lax.rsqrt(lax.optimization_barrier(jnp.mean(values * values, axis=1, keepdims=True)) + 1e-06)
    normed = (values * inv_scale * norm_gain).astype(jnp.bfloat16)
    block_count = TOKENS // TOK_DEV
    block_ids = expert_ids.reshape(block_count, TOK_DEV * TOP)
    onehot = (block_ids[:, :, None] == jnp.arange(EXPERTS, dtype=jnp.int32)[None, None, :]).astype(jnp.int32)
    before = jnp.cumsum(onehot, axis=1) - onehot
    inside = lax.optimization_barrier(jnp.sum(onehot * before, axis=2))
    slot_column = (jnp.arange(block_count, dtype=jnp.int32)[:, None] * CAP + inside).reshape(-1).astype(jnp.int32)
    flat_expert = expert_ids.reshape(-1).astype(jnp.int32)
    token_index = jnp.arange(TOKENS * TOP, dtype=jnp.int32) // TOP
    owners = jnp.full((EXPERTS, block_count * CAP), TOKENS, jnp.int32).at[flat_expert, slot_column].set(token_index)
    slot_gate = jnp.zeros((EXPERTS, block_count * CAP), jnp.float32).at[flat_expert, slot_column].set(gate_weights.reshape(-1))
    padded = jnp.concatenate([normed, jnp.zeros((1, D), jnp.bfloat16)], axis=0)

    def add_expert(total, scan_item):
        owner_rows, gate_slots, gate_mat, up_mat, down_mat = scan_item
        slot_rows = padded[owner_rows]
        gate_act = jnp.dot(slot_rows, gate_mat.T, preferred_element_type=jnp.float32)
        up_act = jnp.dot(slot_rows, up_mat.T, preferred_element_type=jnp.float32)
        hidden = (jax.nn.silu(gate_act) * up_act).astype(jnp.bfloat16)
        result = jnp.dot(hidden, down_mat.T, preferred_element_type=jnp.float32).astype(jnp.bfloat16)
        total = total.at[owner_rows].add(gate_slots[:, None] * result.astype(jnp.float32))
        return (total, None)
    total, _ = lax.scan(add_expert, jnp.zeros((TOKENS + 1, D), jnp.float32), (owners, slot_gate, gate_proj, up_proj, down_proj))
    return total[:TOKENS].astype(jnp.bfloat16)
```

```python
import jax
import jax.numpy as jnp
from jax import lax
from jax.sharding import PartitionSpec as P

D = 4096
EXPERTS = 64
TOP = 8
CAP = 16


epsilon = 1e-06


def earlier_namings(member):
    count = member.shape[-2]
    earlier = jnp.arange(count)[:, None] > jnp.arange(count)[None, :]
    return jnp.einsum(
        "ts,...se->...te",
        earlier.astype(jnp.bfloat16),
        member.astype(jnp.bfloat16),
        preferred_element_type=jnp.float32,
    ).astype(jnp.int32)


def slot_places(expert_ids):
    hit = expert_ids[:, :, None] == jnp.arange(EXPERTS, dtype=jnp.int32)
    before = earlier_namings(jnp.any(hit, axis=1))
    inside = jnp.sum(jnp.where(hit, before[:, None, :], 0), axis=2)
    return (expert_ids * CAP + inside).reshape(-1)


def norm_rows(tokens, norm_gain):
    values = tokens.astype(jnp.float32)
    squares = lax.psum(jnp.sum(values * values, axis=1), "tensor")
    inv_scale = lax.rsqrt(squares / D + epsilon)[:, None]
    width = tokens.shape[1]
    gain_part = lax.dynamic_slice_in_dim(norm_gain, lax.axis_index("tensor") * width, width)
    return (values * inv_scale * gain_part).astype(jnp.bfloat16)


def dispatch_form(tokens, norm_gain, expert_ids, gate_weights, gate_proj, up_proj, down_proj):
    local_experts = gate_proj.shape[0]
    groups = lax.axis_size("expert")
    tok_rows, width = tokens.shape
    places = slot_places(expert_ids)
    owners = (
        jnp.full((EXPERTS * CAP,), tok_rows, jnp.int32)
        .at[places]
        .set(jnp.arange(places.shape[0], dtype=jnp.int32) // TOP)
    )
    normed = norm_rows(tokens, norm_gain)
    padded = jnp.concatenate([normed, jnp.zeros((1, width), jnp.bfloat16)], axis=0)
    dispatched = padded[owners].reshape(groups, local_experts, CAP, width)
    slot_rows = lax.all_gather(
        lax.all_to_all(dispatched, "expert", split_axis=0, concat_axis=0, tiled=True),
        "tensor",
        axis=3,
        tiled=True,
    )
    gate_act = jnp.einsum(
        "slcd,lfd->lfsc", slot_rows, gate_proj, preferred_element_type=jnp.float32
    )
    up_act = jnp.einsum("slcd,lfd->lfsc", slot_rows, up_proj, preferred_element_type=jnp.float32)
    hidden = (jax.nn.silu(gate_act) * up_act).astype(jnp.bfloat16)
    hidden = hidden.reshape(local_experts, hidden.shape[1], groups * CAP)
    hidden_all = lax.all_gather(hidden, "tensor", axis=1, tiled=True)
    hidden_all = hidden_all.reshape(local_experts, hidden_all.shape[1], groups, CAP)
    result = jnp.einsum(
        "lfsc,ldf->slcd", hidden_all, down_proj, preferred_element_type=jnp.float32
    ).astype(jnp.bfloat16)
    returned = lax.all_to_all(result, "expert", split_axis=0, concat_axis=0, tiled=True)
    flat_back = returned.reshape(EXPERTS * CAP, returned.shape[-1])
    picked = flat_back[places].reshape(tok_rows, TOP, -1).astype(jnp.float32)
    return jnp.einsum("tkd,tk->td", picked, gate_weights).astype(jnp.bfloat16)


def gather_form(tokens, norm_gain, expert_ids, gate_weights, gate_proj, up_proj, down_proj):
    local_experts = gate_proj.shape[0]
    groups = lax.axis_size("expert")
    tok_rows = tokens.shape[0]
    ids = lax.all_gather(expert_ids, "expert", axis=0)
    weights = lax.all_gather(gate_weights, "expert", axis=0)
    mine = lax.axis_index("expert") * local_experts + jnp.arange(local_experts, dtype=jnp.int32)
    hit = ids[..., None] == mine
    member = jnp.any(hit, axis=2)
    weight = jnp.sum(jnp.where(hit, weights[..., None], 0.0), axis=2)
    slot = earlier_namings(member) + CAP * jnp.arange(groups)[:, None, None]
    slot = jnp.where(member, slot, -1).reshape(groups * tok_rows, local_experts)
    weight = weight.reshape(groups * tok_rows, local_experts)
    place = slot.T[:, None, :] == jnp.arange(groups * CAP, dtype=jnp.int32)[None, :, None]
    slot_weight = jnp.sum(jnp.where(place, weight.T[:, None, :], 0.0), axis=2)
    place = place.astype(jnp.bfloat16)
    normed = norm_rows(tokens, norm_gain)
    rows = lax.all_gather(lax.all_gather(normed, "expert", axis=0, tiled=True), "tensor", axis=1, tiled=True)
    slot_rows = jnp.einsum("lst,td->lsd", place, rows, preferred_element_type=jnp.float32).astype(jnp.bfloat16)
    gate_act = jnp.einsum("lsd,lfd->lsf", slot_rows, gate_proj, preferred_element_type=jnp.float32)
    up_act = jnp.einsum("lsd,lfd->lsf", slot_rows, up_proj, preferred_element_type=jnp.float32)
    hidden = (jax.nn.silu(gate_act) * up_act).astype(jnp.bfloat16)
    hidden_all = lax.all_gather(hidden, "tensor", axis=2, tiled=True)
    result = jnp.einsum("lsf,ldf->lsd", hidden_all, down_proj, preferred_element_type=jnp.float32)
    result = (result * slot_weight[:, :, None]).astype(jnp.bfloat16)
    partial = jnp.einsum("lst,lsd->td", place, result, preferred_element_type=jnp.float32)
    partial = partial.astype(jnp.bfloat16).reshape(groups, tok_rows, -1)
    parts = lax.all_to_all(partial, "expert", split_axis=0, concat_axis=0, tiled=True)
    return jnp.sum(parts.astype(jnp.float32), axis=0).astype(jnp.bfloat16)


def body(tokens, norm_gain, expert_ids, gate_weights, gate_proj, up_proj, down_proj):
    form = gather_form if tokens.shape[0] < gate_proj.shape[0] * CAP else dispatch_form
    return form(tokens, norm_gain, expert_ids, gate_weights, gate_proj, up_proj, down_proj)


def solution(mesh):
    return jax.shard_map(
        body,
        mesh=mesh,
        in_specs=(
            P(("group", "expert"), "tensor"),
            P(),
            P(("group", "expert"), None),
            P(("group", "expert"), None),
            P("expert", "tensor", None),
            P("expert", "tensor", None),
            P("expert", "tensor", None),
        ),
        out_specs=P(("group", "expert"), "tensor"),
        check_vma=False,
    )
```

```python
import jax
import jax.numpy as jnp
from jax import lax
from jax.experimental import pallas as pl
from jax.experimental.pallas import tpu as pltpu
from jax.sharding import PartitionSpec as P

D = 4096
EXPERTS = 64
TOP = 8
CAP = 16


epsilon = 1e-06


def earlier_namings(member):
    count = member.shape[-2]
    earlier = jnp.arange(count)[:, None] > jnp.arange(count)[None, :]
    return jnp.einsum(
        "ts,...se->...te",
        earlier.astype(jnp.bfloat16),
        member.astype(jnp.bfloat16),
        preferred_element_type=jnp.float32,
    ).astype(jnp.int32)


def slot_places(expert_ids):
    hit = expert_ids[:, :, None] == jnp.arange(EXPERTS, dtype=jnp.int32)
    before = earlier_namings(jnp.any(hit, axis=1))
    inside = jnp.sum(jnp.where(hit, before[:, None, :], 0), axis=2)
    return (expert_ids * CAP + inside).reshape(-1)


def norm_rows(tokens, norm_gain):
    values = tokens.astype(jnp.float32)
    squares = lax.psum(jnp.sum(values * values, axis=1), "tensor")
    inv_scale = lax.rsqrt(squares / D + epsilon)[:, None]
    width = tokens.shape[1]
    gain_part = lax.dynamic_slice_in_dim(norm_gain, lax.axis_index("tensor") * width, width)
    return (values * inv_scale * gain_part).astype(jnp.bfloat16)


def dispatch_form(tokens, norm_gain, expert_ids, gate_weights, gate_proj, up_proj, down_proj):
    local_experts = gate_proj.shape[0]
    groups = lax.axis_size("expert")
    tok_rows, width = tokens.shape
    places = slot_places(expert_ids)
    owners = (
        jnp.full((EXPERTS * CAP,), tok_rows, jnp.int32)
        .at[places]
        .set(jnp.arange(places.shape[0], dtype=jnp.int32) // TOP)
    )
    normed = norm_rows(tokens, norm_gain)
    padded = jnp.concatenate([normed, jnp.zeros((1, width), jnp.bfloat16)], axis=0)
    dispatched = padded[owners].reshape(groups, local_experts, CAP, width)
    slot_rows = lax.all_gather(
        lax.all_to_all(dispatched, "expert", split_axis=0, concat_axis=0, tiled=True),
        "tensor",
        axis=3,
        tiled=True,
    )
    gate_act = jnp.einsum(
        "slcd,lfd->lfsc", slot_rows, gate_proj, preferred_element_type=jnp.float32
    )
    up_act = jnp.einsum("slcd,lfd->lfsc", slot_rows, up_proj, preferred_element_type=jnp.float32)
    hidden = (jax.nn.silu(gate_act) * up_act).astype(jnp.bfloat16)
    hidden = hidden.reshape(local_experts, hidden.shape[1], groups * CAP)
    hidden_all = lax.all_gather(hidden, "tensor", axis=1, tiled=True)
    hidden_all = hidden_all.reshape(local_experts, hidden_all.shape[1], groups, CAP)
    result = jnp.einsum(
        "lfsc,ldf->slcd", hidden_all, down_proj, preferred_element_type=jnp.float32
    ).astype(jnp.bfloat16)
    returned = lax.all_to_all(result, "expert", split_axis=0, concat_axis=0, tiled=True)
    flat_back = returned.reshape(EXPERTS * CAP, returned.shape[-1])
    picked = flat_back[places].reshape(tok_rows, TOP, -1).astype(jnp.float32)
    return jnp.einsum("tkd,tk->td", picked, gate_weights).astype(jnp.bfloat16)


def gather_form(tokens, norm_gain, expert_ids, gate_weights, gate_proj, up_proj, down_proj):
    local_experts = gate_proj.shape[0]
    groups = lax.axis_size("expert")
    tok_rows = tokens.shape[0]
    ids = lax.all_gather(expert_ids, "expert", axis=0)
    weights = lax.all_gather(gate_weights, "expert", axis=0)
    mine = lax.axis_index("expert") * local_experts + jnp.arange(local_experts, dtype=jnp.int32)
    hit = ids[..., None] == mine
    member = jnp.any(hit, axis=2)
    weight = jnp.sum(jnp.where(hit, weights[..., None], 0.0), axis=2)
    slot = earlier_namings(member) + CAP * jnp.arange(groups)[:, None, None]
    slot = jnp.where(member, slot, -1).reshape(groups * tok_rows, local_experts)
    weight = weight.reshape(groups * tok_rows, local_experts)
    place = slot.T[:, None, :] == jnp.arange(groups * CAP, dtype=jnp.int32)[None, :, None]
    slot_weight = jnp.sum(jnp.where(place, weight.T[:, None, :], 0.0), axis=2)
    place = place.astype(jnp.bfloat16)
    normed = norm_rows(tokens, norm_gain)
    rows = lax.all_gather(lax.all_gather(normed, "expert", axis=0, tiled=True), "tensor", axis=1, tiled=True)
    slot_rows = jnp.einsum("lst,td->lsd", place, rows, preferred_element_type=jnp.float32).astype(jnp.bfloat16)
    gate_act = jnp.einsum("lsd,lfd->lsf", slot_rows, gate_proj, preferred_element_type=jnp.float32)
    up_act = jnp.einsum("lsd,lfd->lsf", slot_rows, up_proj, preferred_element_type=jnp.float32)
    hidden = (jax.nn.silu(gate_act) * up_act).astype(jnp.bfloat16)
    hidden_all = lax.all_gather(hidden, "tensor", axis=2, tiled=True)
    result = jnp.einsum("lsf,ldf->lsd", hidden_all, down_proj, preferred_element_type=jnp.float32)
    result = (result * slot_weight[:, :, None]).astype(jnp.bfloat16)
    partial = jnp.einsum("lst,lsd->td", place, result, preferred_element_type=jnp.float32)
    partial = partial.astype(jnp.bfloat16).reshape(groups, tok_rows, -1)
    parts = lax.all_to_all(partial, "expert", split_axis=0, concat_axis=0, tiled=True)
    return jnp.sum(parts.astype(jnp.float32), axis=0).astype(jnp.bfloat16)


NT = (((1,), (1,)), ((), ()))
MESH = pl.DeviceIdType.MESH


def kernel(
    tok_ref, gain_ref, ids_ref, gw_ref, gate_ref, up_ref, down_ref, out_ref,
    raw, xn, info, gu, dn, hid, acc, parts, back,
    gu_sem, dn_sem, tok_send, tok_recv, info_send, info_recv, hid_send, hid_recv, part_send, part_recv,
):
    experts, units, _ = gate_ref.shape
    rows, width = tok_ref.shape
    groups, shards = info.shape[0], raw.shape[0]
    total, pairs = groups * rows, experts // 2
    lanes = info.shape[-1]
    deep_gu, deep_dn = gu.shape[0], dn.shape[0]
    half = groups * CAP
    z, t = lax.axis_index("expert"), lax.axis_index("tensor")
    mate, across, diagonal = t + 1 - 2 * (t % 2), (t + 2) % 4, 3 - t

    def weights(e, slot):
        return [
            pltpu.make_async_copy(gate_ref.at[e], gu.at[slot, 0], gu_sem.at[slot, 0]),
            pltpu.make_async_copy(up_ref.at[e], gu.at[slot, 1], gu_sem.at[slot, 1]),
        ]

    def downs(e, slot):
        return pltpu.make_async_copy(down_ref.at[e], dn.at[slot], dn_sem.at[slot])

    def send(src, dst, ss, rs, **to):
        return pltpu.make_async_remote_copy(
            src_ref=src, dst_ref=dst, send_sem=ss, recv_sem=rs, device_id=to, device_id_type=MESH
        )

    for e in range(deep_gu):
        for c in weights(e, e):
            c.start()
    for e in range(deep_dn):
        downs(e, e).start()

    barrier = pltpu.get_barrier_semaphore()
    for d in range(1, groups):
        pl.semaphore_signal(barrier, inc=1, device_id={"expert": (z + d) % groups}, device_id_type=MESH)
    for peer in (mate, across, diagonal):
        pl.semaphore_signal(barrier, inc=1, device_id={"tensor": peer}, device_id_type=MESH)
    pl.semaphore_wait(barrier, groups + 2)

    def block(shard, d):
        return raw.at[shard, pl.ds(pl.multiple_of((z + groups - d) % groups * rows, rows), rows)]

    first = [
        send(tok_ref, block(t, 0), tok_send.at[0, d], tok_recv.at[0, d], expert=(z + d) % groups)
        for d in range(1, groups)
    ]
    for c in first:
        c.start()
    raw[t, pl.ds(pl.multiple_of(z * rows, rows), rows), :] = tok_ref[...]
    over = [send(block(t, d), block(t, d), tok_send.at[1, d], tok_recv.at[1, d], tensor=across) for d in range(groups)]
    near = [send(block(t, d), block(t, d), tok_send.at[2, d], tok_recv.at[2, d], tensor=mate) for d in range(groups)]
    on = [
        send(block(across, d), block(across, d), tok_send.at[3, d], tok_recv.at[3, d], tensor=mate)
        for d in range(groups)
    ]
    over[0].start()
    near[0].start()

    lane = lax.broadcasted_iota(jnp.int32, (rows, lanes), 1)
    member = jnp.zeros((rows, lanes), jnp.float32)
    weight = jnp.zeros((rows, lanes), jnp.float32)
    for k in range(ids_ref.shape[1]):
        hit = ids_ref[:, k : k + 1] == lane
        member = jnp.where(hit, 1.0, member)
        weight = jnp.where(hit, gw_ref[:, k : k + 1], weight)
    earlier = lax.broadcasted_iota(jnp.int32, (rows, rows), 0) > lax.broadcasted_iota(jnp.int32, (rows, rows), 1)
    before = jnp.dot(
        jnp.where(earlier, 1.0, 0.0).astype(jnp.bfloat16),
        member.astype(jnp.bfloat16),
        preferred_element_type=jnp.float32,
    )
    info[z, 0] = jnp.where(member > 0, before + (z * CAP).astype(jnp.float32), -1000.0)
    info[z, 1] = weight
    told = [
        send(info.at[z], info.at[z], info_send.at[d], info_recv.at[d], expert=(z + d) % groups)
        for d in range(1, groups)
    ]
    for c in told:
        c.start()

    for d in range(1, groups):
        first[d - 1].wait_recv()
        over[d].start()
        near[d].start()
    for d in range(groups):
        over[d].wait_recv()
        on[d].start()
    for c in told:
        c.wait_recv()
    for d in range(groups):
        near[d].wait_recv()
        on[d].wait_recv()

    step = 32

    @pl.loop(0, total // step)
    def _(r):
        at = pl.ds(pl.multiple_of(r * step, step), step)
        values = [raw[s, at, :].astype(jnp.float32) for s in range(shards)]
        squares = sum(jnp.sum(v * v, axis=1, keepdims=True) for v in values)
        inv_scale = lax.rsqrt(squares / (shards * width) + epsilon)
        for s in range(shards):
            xn[s, at, :] = (values[s] * inv_scale * gain_ref[s : s + 1, :]).astype(jnp.bfloat16)

    def column(which, e):
        table = info[:, which].reshape(total, lanes)
        here = lax.broadcasted_iota(jnp.int32, (total, lanes), 1) == z * experts + e
        return jnp.sum(jnp.where(here, table, 0.0), axis=1, keepdims=True)

    def place(e, side):
        at = lax.broadcasted_iota(jnp.int32, (total, 2 * half), 1).astype(jnp.float32)
        return jnp.where(column(0, e) + float(side * half) == at, 1.0, 0.0).astype(jnp.bfloat16)

    def part_of_hidden(p):
        return hid.at[p, pl.ds(pl.multiple_of(t * units, units), units)]

    def tell(p):
        return [
            send(part_of_hidden(p), part_of_hidden(p), hid_send.at[p, i], hid_recv.at[p, i], tensor=peer)
            for i, peer in enumerate((mate, across, diagonal))
        ]

    @pl.loop(0, pairs)
    def _(p):
        both = jnp.zeros((units, 2 * half), jnp.float32)
        for side in range(2):
            e = 2 * p + side
            slot = e % deep_gu
            for c in weights(e, slot):
                c.wait()
            acts = []
            for m in range(2):
                act = jnp.zeros((units, total), jnp.float32)
                for s in range(shards):
                    act += lax.dot_general(
                        gu[slot, m, :, s * width : (s + 1) * width], xn[s], NT, preferred_element_type=jnp.float32
                    )
                acts.append(act)

            @pl.when(e + deep_gu < experts)
            def _():
                for c in weights(e + deep_gu, slot):
                    c.start()

            hidden = (acts[0] / (1.0 + jnp.exp(-acts[0])) * acts[1]).astype(jnp.bfloat16)
            both += jnp.dot(hidden, place(e, side), preferred_element_type=jnp.float32)
        hid[p, pl.ds(pl.multiple_of(t * units, units), units), :] = both.astype(jnp.bfloat16)
        for c in tell(p):
            c.start()

    acc[...] = jnp.zeros_like(acc)

    @pl.loop(0, pairs)
    def _(p):
        for c in tell(p):
            c.wait()
        for side in range(2):
            e = 2 * p + side
            slot = e % deep_dn
            downs(e, slot).wait()
            spread = lax.dot_general(place(e, side), hid[p], NT, preferred_element_type=jnp.float32)
            spread = (spread * column(1, e)).astype(jnp.bfloat16)
            acc[...] += lax.dot_general(spread, dn[slot], NT, preferred_element_type=jnp.float32)

            @pl.when(e + deep_dn < experts)
            def _():
                downs(e + deep_dn, slot).start()

    for b in range(groups):
        parts[b] = acc[b * rows : (b + 1) * rows, :].astype(jnp.bfloat16)
    shares = [
        send(parts.at[(z + d) % groups], back.at[d], part_send.at[d], part_recv.at[d], expert=(z + d) % groups)
        for d in range(1, groups)
    ]
    for c in shares:
        c.start()
    result = acc[pl.ds(pl.multiple_of(z * rows, rows), rows), :]
    for d, c in enumerate(shares, 1):
        c.wait_recv()
        result += back[d].astype(jnp.float32)
    out_ref[...] = result.astype(jnp.bfloat16)
    for c in first + over + near + on + told + shares:
        c.wait_send()


def kernel_form(tokens, norm_gain, expert_ids, gate_weights, gate_proj, up_proj, down_proj):
    groups, shards = lax.axis_size("expert"), lax.axis_size("tensor")
    rows, width = tokens.shape
    experts, units, features = gate_proj.shape
    out_width = down_proj.shape[1]
    total, pairs, lanes = groups * rows, experts // 2, -(-EXPERTS // 128) * 128
    deep_gu, deep_dn = min(experts, 8), min(experts, 10)
    vmem, hbm = pl.BlockSpec(memory_space=pltpu.VMEM), pl.BlockSpec(memory_space=pl.ANY)
    dma = pltpu.SemaphoreType.DMA
    flops = 2 * total * experts * (2 * units * features + out_width * down_proj.shape[2])
    return pl.pallas_call(
        kernel,
        out_shape=jax.ShapeDtypeStruct((rows, out_width), jnp.bfloat16),
        in_specs=[vmem] * 4 + [hbm] * 3,
        out_specs=vmem,
        scratch_shapes=[
            pltpu.VMEM((shards, total, width), jnp.bfloat16),
            pltpu.VMEM((shards, total, width), jnp.bfloat16),
            pltpu.VMEM((groups, 2, rows, lanes), jnp.float32),
            pltpu.VMEM((deep_gu, 2, units, features), jnp.bfloat16),
            pltpu.VMEM((deep_dn,) + down_proj.shape[1:], jnp.bfloat16),
            pltpu.VMEM((pairs, shards * units, 2 * groups * CAP), jnp.bfloat16),
            pltpu.VMEM((total, out_width), jnp.float32),
            pltpu.VMEM((groups, rows, out_width), jnp.bfloat16),
            pltpu.VMEM((groups, rows, out_width), jnp.bfloat16),
            dma((deep_gu, 2)),
            dma((deep_dn,)),
            dma((4, groups)),
            dma((4, groups)),
            dma((groups,)),
            dma((groups,)),
            dma((pairs, 3)),
            dma((pairs, 3)),
            dma((groups,)),
            dma((groups,)),
        ],
        compiler_params=pltpu.CompilerParams(
            collective_id=0, has_side_effects=True, vmem_limit_bytes=58 * 2**20
        ),
        cost_estimate=pl.CostEstimate(flops=flops, bytes_accessed=3 * 2 * gate_proj.size, transcendentals=0),
    )(tokens, norm_gain.reshape(shards, width), expert_ids, gate_weights, gate_proj, up_proj, down_proj)


def body(tokens, norm_gain, expert_ids, gate_weights, gate_proj, up_proj, down_proj):
    form = dispatch_form
    if tokens.shape[0] < gate_proj.shape[0] * CAP:
        form = gather_form
        if lax.axis_size("tensor") == 4 and gate_proj.shape[0] % 2 == 0:
            form = kernel_form
    return form(tokens, norm_gain, expert_ids, gate_weights, gate_proj, up_proj, down_proj)


def solution(mesh):
    return jax.shard_map(
        body,
        mesh=mesh,
        in_specs=(
            P(("group", "expert"), "tensor"),
            P(),
            P(("group", "expert"), None),
            P(("group", "expert"), None),
            P("expert", "tensor", None),
            P("expert", "tensor", None),
            P("expert", "tensor", None),
        ),
        out_specs=P(("group", "expert"), "tensor"),
        check_vma=False,
    )
```

```python
import jax
import jax.numpy as jnp
from jax import lax
from jax.experimental import pallas as pl
from jax.experimental.pallas import tpu as pltpu
from jax.sharding import PartitionSpec as P

D = 4096
EXPERTS = 64
TOP = 8
CAP = 16


epsilon = 1e-06


def earlier_namings(member):
    count = member.shape[-2]
    earlier = jnp.arange(count)[:, None] > jnp.arange(count)[None, :]
    return jnp.einsum(
        "ts,...se->...te",
        earlier.astype(jnp.bfloat16),
        member.astype(jnp.bfloat16),
        preferred_element_type=jnp.float32,
    ).astype(jnp.int32)


def slot_places(expert_ids):
    hit = expert_ids[:, :, None] == jnp.arange(EXPERTS, dtype=jnp.int32)
    before = earlier_namings(jnp.any(hit, axis=1))
    inside = jnp.sum(jnp.where(hit, before[:, None, :], 0), axis=2)
    return (expert_ids * CAP + inside).reshape(-1)


def norm_rows(tokens, norm_gain):
    values = tokens.astype(jnp.float32)
    squares = lax.psum(jnp.sum(values * values, axis=1), "tensor")
    inv_scale = lax.rsqrt(squares / D + epsilon)[:, None]
    width = tokens.shape[1]
    gain_part = lax.dynamic_slice_in_dim(norm_gain, lax.axis_index("tensor") * width, width)
    return (values * inv_scale * gain_part).astype(jnp.bfloat16)


def dispatch_form(tokens, norm_gain, expert_ids, gate_weights, gate_proj, up_proj, down_proj):
    local_experts = gate_proj.shape[0]
    groups = lax.axis_size("expert")
    tok_rows, width = tokens.shape
    places = slot_places(expert_ids)
    owners = (
        jnp.full((EXPERTS * CAP,), tok_rows, jnp.int32)
        .at[places]
        .set(jnp.arange(places.shape[0], dtype=jnp.int32) // TOP)
    )
    normed = norm_rows(tokens, norm_gain)
    padded = jnp.concatenate([normed, jnp.zeros((1, width), jnp.bfloat16)], axis=0)
    dispatched = padded[owners].reshape(groups, local_experts, CAP, width)
    slot_rows = lax.all_gather(
        lax.all_to_all(dispatched, "expert", split_axis=0, concat_axis=0, tiled=True),
        "tensor",
        axis=3,
        tiled=True,
    )
    gate_act = jnp.einsum(
        "slcd,lfd->lfsc", slot_rows, gate_proj, preferred_element_type=jnp.float32
    )
    up_act = jnp.einsum("slcd,lfd->lfsc", slot_rows, up_proj, preferred_element_type=jnp.float32)
    hidden = (jax.nn.silu(gate_act) * up_act).astype(jnp.bfloat16)
    hidden = hidden.reshape(local_experts, hidden.shape[1], groups * CAP)
    hidden_all = lax.all_gather(hidden, "tensor", axis=1, tiled=True)
    hidden_all = hidden_all.reshape(local_experts, hidden_all.shape[1], groups, CAP)
    result = jnp.einsum(
        "lfsc,ldf->slcd", hidden_all, down_proj, preferred_element_type=jnp.float32
    ).astype(jnp.bfloat16)
    returned = lax.all_to_all(result, "expert", split_axis=0, concat_axis=0, tiled=True)
    flat_back = returned.reshape(EXPERTS * CAP, returned.shape[-1])
    picked = flat_back[places].reshape(tok_rows, TOP, -1).astype(jnp.float32)
    return jnp.einsum("tkd,tk->td", picked, gate_weights).astype(jnp.bfloat16)


def gather_form(tokens, norm_gain, expert_ids, gate_weights, gate_proj, up_proj, down_proj):
    local_experts = gate_proj.shape[0]
    groups = lax.axis_size("expert")
    tok_rows = tokens.shape[0]
    ids = lax.all_gather(expert_ids, "expert", axis=0)
    weights = lax.all_gather(gate_weights, "expert", axis=0)
    mine = lax.axis_index("expert") * local_experts + jnp.arange(local_experts, dtype=jnp.int32)
    hit = ids[..., None] == mine
    member = jnp.any(hit, axis=2)
    weight = jnp.sum(jnp.where(hit, weights[..., None], 0.0), axis=2)
    slot = earlier_namings(member) + CAP * jnp.arange(groups)[:, None, None]
    slot = jnp.where(member, slot, -1).reshape(groups * tok_rows, local_experts)
    weight = weight.reshape(groups * tok_rows, local_experts)
    place = slot.T[:, None, :] == jnp.arange(groups * CAP, dtype=jnp.int32)[None, :, None]
    slot_weight = jnp.sum(jnp.where(place, weight.T[:, None, :], 0.0), axis=2)
    place = place.astype(jnp.bfloat16)
    normed = norm_rows(tokens, norm_gain)
    rows = lax.all_gather(lax.all_gather(normed, "expert", axis=0, tiled=True), "tensor", axis=1, tiled=True)
    slot_rows = jnp.einsum("lst,td->lsd", place, rows, preferred_element_type=jnp.float32).astype(jnp.bfloat16)
    gate_act = jnp.einsum("lsd,lfd->lsf", slot_rows, gate_proj, preferred_element_type=jnp.float32)
    up_act = jnp.einsum("lsd,lfd->lsf", slot_rows, up_proj, preferred_element_type=jnp.float32)
    hidden = (jax.nn.silu(gate_act) * up_act).astype(jnp.bfloat16)
    hidden_all = lax.all_gather(hidden, "tensor", axis=2, tiled=True)
    result = jnp.einsum("lsf,ldf->lsd", hidden_all, down_proj, preferred_element_type=jnp.float32)
    result = (result * slot_weight[:, :, None]).astype(jnp.bfloat16)
    partial = jnp.einsum("lst,lsd->td", place, result, preferred_element_type=jnp.float32)
    partial = partial.astype(jnp.bfloat16).reshape(groups, tok_rows, -1)
    parts = lax.all_to_all(partial, "expert", split_axis=0, concat_axis=0, tiled=True)
    return jnp.sum(parts.astype(jnp.float32), axis=0).astype(jnp.bfloat16)


NT = (((1,), (1,)), ((), ()))
MESH = pl.DeviceIdType.MESH


def kernel(
    tok_ref, gain_ref, ids_ref, gw_ref, gate_ref, up_ref, down_ref, out_ref,
    raw, xn, info, gu, dn, hid, spread, acc, parts, back,
    gu_sem, dn_sem, tok_send, tok_recv, info_send, info_recv, hid_send, hid_recv, part_send, part_recv,
):
    experts, units, _ = gate_ref.shape
    rows, width = tok_ref.shape
    groups, shards = info.shape[0], raw.shape[0]
    total, pairs = groups * rows, experts // 2
    lanes = info.shape[-1]
    deep_gu, deep_dn = gu.shape[0], dn.shape[0]
    half = groups * CAP
    z, t = lax.axis_index("expert"), lax.axis_index("tensor")
    mate, across, diagonal = t + 1 - 2 * (t % 2), (t + 2) % 4, 3 - t

    depth, part = down_ref.shape[2], acc.shape[2]

    def weights(p, slot):
        return [
            pltpu.make_async_copy(ref.at[2 * p + side], gu.at[slot, side, m], gu_sem.at[slot, side, m])
            for side in range(2)
            for m, ref in enumerate((gate_ref, up_ref))
        ]

    def downs(unit, slot):
        h, p = unit // pairs, unit % pairs
        features = pl.ds(pl.multiple_of(h * part, part), part)
        return [
            pltpu.make_async_copy(
                down_ref.at[2 * p + side, features],
                dn.at[slot, :, pl.ds(side * depth, depth)],
                dn_sem.at[slot, side],
            )
            for side in range(2)
        ]

    def send(src, dst, ss, rs, **to):
        return pltpu.make_async_remote_copy(
            src_ref=src, dst_ref=dst, send_sem=ss, recv_sem=rs, device_id=to, device_id_type=MESH
        )

    for e in range(deep_gu):
        for c in weights(e, e):
            c.start()
    for e in range(deep_dn):
        for c in downs(e, e):
            c.start()

    barrier = pltpu.get_barrier_semaphore()
    for d in range(1, groups):
        pl.semaphore_signal(barrier, inc=1, device_id={"expert": (z + d) % groups}, device_id_type=MESH)
    for peer in (mate, across, diagonal):
        pl.semaphore_signal(barrier, inc=1, device_id={"tensor": peer}, device_id_type=MESH)
    pl.semaphore_wait(barrier, groups + 2)

    def block(shard, d):
        return raw.at[shard, pl.ds(pl.multiple_of((z + groups - d) % groups * rows, rows), rows)]

    first = [
        send(tok_ref, block(t, 0), tok_send.at[0, d], tok_recv.at[0, d], expert=(z + d) % groups)
        for d in range(1, groups)
    ]
    for c in first:
        c.start()
    raw[t, pl.ds(pl.multiple_of(z * rows, rows), rows), :] = tok_ref[...]
    over = [send(block(t, d), block(t, d), tok_send.at[1, d], tok_recv.at[1, d], tensor=across) for d in range(groups)]
    near = [send(block(t, d), block(t, d), tok_send.at[2, d], tok_recv.at[2, d], tensor=mate) for d in range(groups)]
    on = [
        send(block(across, d), block(across, d), tok_send.at[3, d], tok_recv.at[3, d], tensor=mate)
        for d in range(groups)
    ]
    over[0].start()
    near[0].start()

    lane = lax.broadcasted_iota(jnp.int32, (rows, lanes), 1)
    member = jnp.zeros((rows, lanes), jnp.float32)
    weight = jnp.zeros((rows, lanes), jnp.float32)
    for k in range(ids_ref.shape[1]):
        hit = ids_ref[:, k : k + 1] == lane
        member = jnp.where(hit, 1.0, member)
        weight = jnp.where(hit, gw_ref[:, k : k + 1], weight)
    earlier = lax.broadcasted_iota(jnp.int32, (rows, rows), 0) > lax.broadcasted_iota(jnp.int32, (rows, rows), 1)
    before = jnp.dot(
        jnp.where(earlier, 1.0, 0.0).astype(jnp.bfloat16),
        member.astype(jnp.bfloat16),
        preferred_element_type=jnp.float32,
    )
    info[z, 0] = jnp.where(member > 0, before + (z * CAP).astype(jnp.float32), -1000.0)
    info[z, 1] = weight
    told = [
        send(info.at[z], info.at[z], info_send.at[d], info_recv.at[d], expert=(z + d) % groups)
        for d in range(1, groups)
    ]
    for c in told:
        c.start()

    for d in range(1, groups):
        first[d - 1].wait_recv()
        over[d].start()
        near[d].start()
    for d in range(groups):
        over[d].wait_recv()
        on[d].start()
    for c in told:
        c.wait_recv()
    for d in range(groups):
        near[d].wait_recv()
        on[d].wait_recv()

    step = 32

    @pl.loop(0, total // step)
    def _(r):
        at = pl.ds(pl.multiple_of(r * step, step), step)
        values = [raw[s, at, :].astype(jnp.float32) for s in range(shards)]
        squares = sum(jnp.sum(v * v, axis=1, keepdims=True) for v in values)
        inv_scale = lax.rsqrt(squares / (shards * width) + epsilon)
        for s in range(shards):
            xn[at, s * width : (s + 1) * width] = (values[s] * inv_scale * gain_ref[s : s + 1, :]).astype(jnp.bfloat16)

    def column(which, e):
        table = info[:, which].reshape(total, lanes)
        here = lax.broadcasted_iota(jnp.int32, (total, lanes), 1) == z * experts + e
        return jnp.sum(jnp.where(here, table, 0.0), axis=1, keepdims=True)

    def place(e, side):
        at = lax.broadcasted_iota(jnp.int32, (total, 2 * half), 1).astype(jnp.float32)
        return jnp.where(column(0, e) + float(side * half) == at, 1.0, 0.0).astype(jnp.bfloat16)

    def part_of_hidden(p):
        return hid.at[p, pl.ds(pl.multiple_of(t * units, units), units)]

    def tell(p):
        return [
            send(part_of_hidden(p), part_of_hidden(p), hid_send.at[p, i], hid_recv.at[p, i], tensor=peer)
            for i, peer in enumerate((mate, across, diagonal))
        ]

    @pl.loop(0, pairs)
    def _(p):
        slot = p % deep_gu
        for c in weights(p, slot):
            c.wait()
        acts = lax.dot_general(
            gu[slot].reshape(4 * units, shards * width), xn[...], NT, preferred_element_type=jnp.float32
        )

        @pl.when(p + deep_gu < pairs)
        def _():
            for c in weights(p + deep_gu, slot):
                c.start()

        both = jnp.zeros((units, 2 * half), jnp.float32)
        for side in range(2):
            gate = acts[2 * side * units : (2 * side + 1) * units]
            up = acts[(2 * side + 1) * units : (2 * side + 2) * units]
            hidden = (gate / (1.0 + jnp.exp(-gate)) * up).astype(jnp.bfloat16)
            both += jnp.dot(hidden, place(2 * p + side, side), preferred_element_type=jnp.float32)
        hid[p, pl.ds(pl.multiple_of(t * units, units), units), :] = both.astype(jnp.bfloat16)
        for c in tell(p):
            c.start()

    def shares(h):
        return [
            send(
                parts.at[h, (z + d) % groups], back.at[h, d], part_send.at[h, d], part_recv.at[h, d],
                expert=(z + d) % groups,
            )
            for d in range(1, groups)
        ]

    for h in range(2):
        acc[h] = jnp.zeros_like(acc[h])

        @pl.loop(0, pairs)
        def _(p):
            if h == 0:
                for c in tell(p):
                    c.wait()
                for side in range(2):
                    e = 2 * p + side
                    rows_of = lax.dot_general(place(e, side), hid[p], NT, preferred_element_type=jnp.float32)
                    spread[p, :, side * depth : (side + 1) * depth] = (rows_of * column(1, e)).astype(jnp.bfloat16)
            unit = h * pairs + p
            slot = unit % deep_dn
            for c in downs(unit, slot):
                c.wait()
            acc[h] += lax.dot_general(spread[p], dn[slot], NT, preferred_element_type=jnp.float32)

            @pl.when(unit + deep_dn < 2 * pairs)
            def _():
                for c in downs(unit + deep_dn, slot):
                    c.start()

        for b in range(groups):
            parts[h, b] = acc[h, b * rows : (b + 1) * rows, :].astype(jnp.bfloat16)
        for c in shares(h):
            c.start()

    for h in range(2):
        result = acc[h, pl.ds(pl.multiple_of(z * rows, rows), rows), :]
        for d, c in enumerate(shares(h), 1):
            c.wait_recv()
            result += back[h, d].astype(jnp.float32)
        out_ref[:, h * part : (h + 1) * part] = result.astype(jnp.bfloat16)
    for c in first + over + near + on + told + shares(0) + shares(1):
        c.wait_send()


def kernel_form(tokens, norm_gain, expert_ids, gate_weights, gate_proj, up_proj, down_proj):
    groups, shards = lax.axis_size("expert"), lax.axis_size("tensor")
    rows, width = tokens.shape
    experts, units, features = gate_proj.shape
    out_width = down_proj.shape[1]
    total, pairs, lanes = groups * rows, experts // 2, -(-EXPERTS // 128) * 128
    deep_gu, deep_dn, part = min(pairs, 4), min(2 * pairs, 8), out_width // 2
    vmem, hbm = pl.BlockSpec(memory_space=pltpu.VMEM), pl.BlockSpec(memory_space=pl.ANY)
    dma = pltpu.SemaphoreType.DMA
    flops = 2 * total * experts * (2 * units * features + out_width * down_proj.shape[2])
    return pl.pallas_call(
        kernel,
        out_shape=jax.ShapeDtypeStruct((rows, out_width), jnp.bfloat16),
        in_specs=[vmem] * 4 + [hbm] * 3,
        out_specs=vmem,
        scratch_shapes=[
            pltpu.VMEM((shards, total, width), jnp.bfloat16),
            pltpu.VMEM((total, shards * width), jnp.bfloat16),
            pltpu.VMEM((groups, 2, rows, lanes), jnp.float32),
            pltpu.VMEM((deep_gu, 2, 2, units, features), jnp.bfloat16),
            pltpu.VMEM((deep_dn, part, 2 * down_proj.shape[2]), jnp.bfloat16),
            pltpu.VMEM((pairs, shards * units, 2 * groups * CAP), jnp.bfloat16),
            pltpu.VMEM((pairs, total, 2 * down_proj.shape[2]), jnp.bfloat16),
            pltpu.VMEM((2, total, part), jnp.float32),
            pltpu.VMEM((2, groups, rows, part), jnp.bfloat16),
            pltpu.VMEM((2, groups, rows, part), jnp.bfloat16),
            dma((deep_gu, 2, 2)),
            dma((deep_dn, 2)),
            dma((4, groups)),
            dma((4, groups)),
            dma((groups,)),
            dma((groups,)),
            dma((pairs, 3)),
            dma((pairs, 3)),
            dma((2, groups)),
            dma((2, groups)),
        ],
        compiler_params=pltpu.CompilerParams(
            collective_id=0, has_side_effects=True, vmem_limit_bytes=58 * 2**20
        ),
        cost_estimate=pl.CostEstimate(flops=flops, bytes_accessed=3 * 2 * gate_proj.size, transcendentals=0),
    )(tokens, norm_gain.reshape(shards, width), expert_ids, gate_weights, gate_proj, up_proj, down_proj)


def body(tokens, norm_gain, expert_ids, gate_weights, gate_proj, up_proj, down_proj):
    form = dispatch_form
    if tokens.shape[0] < gate_proj.shape[0] * CAP:
        form = gather_form
        if lax.axis_size("tensor") == 4 and gate_proj.shape[0] % 2 == 0:
            form = kernel_form
    return form(tokens, norm_gain, expert_ids, gate_weights, gate_proj, up_proj, down_proj)


def solution(mesh):
    return jax.shard_map(
        body,
        mesh=mesh,
        in_specs=(
            P(("group", "expert"), "tensor"),
            P(),
            P(("group", "expert"), None),
            P(("group", "expert"), None),
            P("expert", "tensor", None),
            P("expert", "tensor", None),
            P("expert", "tensor", None),
        ),
        out_specs=P(("group", "expert"), "tensor"),
        check_vma=False,
    )
```

```python
import jax
import jax.numpy as jnp
from jax import lax
from jax.experimental import pallas as pl
from jax.experimental.pallas import tpu as pltpu
from jax.sharding import PartitionSpec as P

D = 4096
EXPERTS = 64
TOP = 8
CAP = 16


epsilon = 1e-06


def earlier_namings(member):
    count = member.shape[-2]
    earlier = jnp.arange(count)[:, None] > jnp.arange(count)[None, :]
    return jnp.einsum(
        "ts,...se->...te",
        earlier.astype(jnp.bfloat16),
        member.astype(jnp.bfloat16),
        preferred_element_type=jnp.float32,
    ).astype(jnp.int32)


def slot_places(expert_ids):
    hit = expert_ids[:, :, None] == jnp.arange(EXPERTS, dtype=jnp.int32)
    before = earlier_namings(jnp.any(hit, axis=1))
    inside = jnp.sum(jnp.where(hit, before[:, None, :], 0), axis=2)
    return (expert_ids * CAP + inside).reshape(-1)


def norm_rows(tokens, norm_gain):
    values = tokens.astype(jnp.float32)
    squares = lax.psum(jnp.sum(values * values, axis=1), "tensor")
    inv_scale = lax.rsqrt(squares / D + epsilon)[:, None]
    width = tokens.shape[1]
    gain_part = lax.dynamic_slice_in_dim(norm_gain, lax.axis_index("tensor") * width, width)
    return (values * inv_scale * gain_part).astype(jnp.bfloat16)


def dispatch_form(tokens, norm_gain, expert_ids, gate_weights, gate_proj, up_proj, down_proj):
    local_experts = gate_proj.shape[0]
    groups = lax.axis_size("expert")
    tok_rows, width = tokens.shape
    places = slot_places(expert_ids)
    owners = (
        jnp.full((EXPERTS * CAP,), tok_rows, jnp.int32)
        .at[places]
        .set(jnp.arange(places.shape[0], dtype=jnp.int32) // TOP)
    )
    normed = norm_rows(tokens, norm_gain)
    padded = jnp.concatenate([normed, jnp.zeros((1, width), jnp.bfloat16)], axis=0)
    dispatched = padded[owners].reshape(groups, local_experts, CAP, width)
    slot_rows = lax.all_gather(
        lax.all_to_all(dispatched, "expert", split_axis=0, concat_axis=0, tiled=True),
        "tensor",
        axis=3,
        tiled=True,
    )
    gate_act = jnp.einsum(
        "slcd,lfd->lfsc", slot_rows, gate_proj, preferred_element_type=jnp.float32
    )
    up_act = jnp.einsum("slcd,lfd->lfsc", slot_rows, up_proj, preferred_element_type=jnp.float32)
    hidden = (jax.nn.silu(gate_act) * up_act).astype(jnp.bfloat16)
    hidden = hidden.reshape(local_experts, hidden.shape[1], groups * CAP)
    hidden_all = lax.all_gather(hidden, "tensor", axis=1, tiled=True)
    hidden_all = hidden_all.reshape(local_experts, hidden_all.shape[1], groups, CAP)
    result = jnp.einsum(
        "lfsc,ldf->slcd", hidden_all, down_proj, preferred_element_type=jnp.float32
    ).astype(jnp.bfloat16)
    returned = lax.all_to_all(result, "expert", split_axis=0, concat_axis=0, tiled=True)
    flat_back = returned.reshape(EXPERTS * CAP, returned.shape[-1])
    picked = flat_back[places].reshape(tok_rows, TOP, -1).astype(jnp.float32)
    return jnp.einsum("tkd,tk->td", picked, gate_weights).astype(jnp.bfloat16)


def gather_form(tokens, norm_gain, expert_ids, gate_weights, gate_proj, up_proj, down_proj):
    local_experts = gate_proj.shape[0]
    groups = lax.axis_size("expert")
    tok_rows = tokens.shape[0]
    ids = lax.all_gather(expert_ids, "expert", axis=0)
    weights = lax.all_gather(gate_weights, "expert", axis=0)
    mine = lax.axis_index("expert") * local_experts + jnp.arange(local_experts, dtype=jnp.int32)
    hit = ids[..., None] == mine
    member = jnp.any(hit, axis=2)
    weight = jnp.sum(jnp.where(hit, weights[..., None], 0.0), axis=2)
    slot = earlier_namings(member) + CAP * jnp.arange(groups)[:, None, None]
    slot = jnp.where(member, slot, -1).reshape(groups * tok_rows, local_experts)
    weight = weight.reshape(groups * tok_rows, local_experts)
    place = slot.T[:, None, :] == jnp.arange(groups * CAP, dtype=jnp.int32)[None, :, None]
    slot_weight = jnp.sum(jnp.where(place, weight.T[:, None, :], 0.0), axis=2)
    place = place.astype(jnp.bfloat16)
    normed = norm_rows(tokens, norm_gain)
    rows = lax.all_gather(lax.all_gather(normed, "expert", axis=0, tiled=True), "tensor", axis=1, tiled=True)
    slot_rows = jnp.einsum("lst,td->lsd", place, rows, preferred_element_type=jnp.float32).astype(jnp.bfloat16)
    gate_act = jnp.einsum("lsd,lfd->lsf", slot_rows, gate_proj, preferred_element_type=jnp.float32)
    up_act = jnp.einsum("lsd,lfd->lsf", slot_rows, up_proj, preferred_element_type=jnp.float32)
    hidden = (jax.nn.silu(gate_act) * up_act).astype(jnp.bfloat16)
    hidden_all = lax.all_gather(hidden, "tensor", axis=2, tiled=True)
    result = jnp.einsum("lsf,ldf->lsd", hidden_all, down_proj, preferred_element_type=jnp.float32)
    result = (result * slot_weight[:, :, None]).astype(jnp.bfloat16)
    partial = jnp.einsum("lst,lsd->td", place, result, preferred_element_type=jnp.float32)
    partial = partial.astype(jnp.bfloat16).reshape(groups, tok_rows, -1)
    parts = lax.all_to_all(partial, "expert", split_axis=0, concat_axis=0, tiled=True)
    return jnp.sum(parts.astype(jnp.float32), axis=0).astype(jnp.bfloat16)


NT = (((1,), (1,)), ((), ()))
MESH = pl.DeviceIdType.MESH


def kernel(
    tok_ref, gain_ref, ids_ref, gw_ref, gate_ref, up_ref, down_ref, out_ref,
    raw, xn, info, gu, dn, hid, spread, acc, parts, back,
    gu_sem, dn_sem, tok_send, tok_recv, info_send, info_recv, hid_send, hid_recv, part_send, part_recv,
):
    experts, units, _ = gate_ref.shape
    rows, width = tok_ref.shape
    groups, shards = info.shape[0], raw.shape[0]
    total, pairs = groups * rows, experts // 2
    lanes = info.shape[-1]
    deep_gu, deep_dn = gu.shape[0], dn.shape[0]
    half = groups * CAP
    z, t = lax.axis_index("expert"), lax.axis_index("tensor")
    mate, across, diagonal = t + 1 - 2 * (t % 2), (t + 2) % 4, 3 - t

    depth, part = down_ref.shape[2], acc.shape[2]

    def weights(p, slot):
        return [
            pltpu.make_async_copy(ref.at[2 * p + side], gu.at[slot, side, m], gu_sem.at[slot, side, m])
            for side in range(2)
            for m, ref in enumerate((gate_ref, up_ref))
        ]

    def downs(unit, slot):
        h, p = unit // pairs, unit % pairs
        features = pl.ds(pl.multiple_of(h * part, part), part)
        return [
            pltpu.make_async_copy(
                down_ref.at[2 * p + side, features],
                dn.at[slot, :, pl.ds(side * depth, depth)],
                dn_sem.at[slot, side],
            )
            for side in range(2)
        ]

    def send(src, dst, ss, rs, **to):
        return pltpu.make_async_remote_copy(
            src_ref=src, dst_ref=dst, send_sem=ss, recv_sem=rs, device_id=to, device_id_type=MESH
        )

    ahead = [weights(p, p) for p in range(deep_gu)] + [downs(u, u) for u in range(deep_dn)]

    def prefetch(count):
        for _ in range(min(count, len(ahead))):
            for c in ahead.pop(0):
                c.start()

    prefetch(1)
    barrier = pltpu.get_barrier_semaphore()
    for d in range(1, groups):
        pl.semaphore_signal(barrier, inc=1, device_id={"expert": (z + d) % groups}, device_id_type=MESH)
    for peer in (mate, across, diagonal):
        pl.semaphore_signal(barrier, inc=1, device_id={"tensor": peer}, device_id_type=MESH)
    pl.semaphore_wait(barrier, groups + 2)

    def block(shard, d):
        return raw.at[shard, pl.ds(pl.multiple_of((z + groups - d) % groups * rows, rows), rows)]

    first = [
        send(tok_ref, block(t, 0), tok_send.at[0, d], tok_recv.at[0, d], expert=(z + d) % groups)
        for d in range(1, groups)
    ]
    for c in first:
        c.start()
    raw[t, pl.ds(pl.multiple_of(z * rows, rows), rows), :] = tok_ref[...]
    over = [send(block(t, d), block(t, d), tok_send.at[1, d], tok_recv.at[1, d], tensor=across) for d in range(groups)]
    near = [send(block(t, d), block(t, d), tok_send.at[2, d], tok_recv.at[2, d], tensor=mate) for d in range(groups)]
    on = [
        send(block(across, d), block(across, d), tok_send.at[3, d], tok_recv.at[3, d], tensor=mate)
        for d in range(groups)
    ]
    over[0].start()
    near[0].start()
    prefetch(1)

    lane = lax.broadcasted_iota(jnp.int32, (rows, lanes), 1)
    member = jnp.zeros((rows, lanes), jnp.float32)
    weight = jnp.zeros((rows, lanes), jnp.float32)
    for k in range(ids_ref.shape[1]):
        hit = ids_ref[:, k : k + 1] == lane
        member = jnp.where(hit, 1.0, member)
        weight = jnp.where(hit, gw_ref[:, k : k + 1], weight)
    earlier = lax.broadcasted_iota(jnp.int32, (rows, rows), 0) > lax.broadcasted_iota(jnp.int32, (rows, rows), 1)
    before = jnp.dot(
        jnp.where(earlier, 1.0, 0.0).astype(jnp.bfloat16),
        member.astype(jnp.bfloat16),
        preferred_element_type=jnp.float32,
    )
    info[z, 0] = jnp.where(member > 0, before + (z * CAP).astype(jnp.float32), -1000.0)
    info[z, 1] = weight
    told = [
        send(info.at[z], info.at[z], info_send.at[d], info_recv.at[d], expert=(z + d) % groups)
        for d in range(1, groups)
    ]
    for c in told:
        c.start()

    step = 32

    def norm(d):
        near[d].wait_recv()
        on[d].wait_recv()
        base = (z + groups - d) % groups * rows

        @pl.loop(0, rows // step)
        def _(r):
            at = pl.ds(pl.multiple_of(base + r * step, step), step)
            values = [raw[s, at, :].astype(jnp.float32) for s in range(shards)]
            squares = sum(jnp.sum(v * v, axis=1, keepdims=True) for v in values)
            inv_scale = lax.rsqrt(squares / (shards * width) + epsilon)
            for s in range(shards):
                xn[at, s * width : (s + 1) * width] = (values[s] * inv_scale * gain_ref[s : s + 1, :]).astype(
                    jnp.bfloat16
                )

    for d in range(1, groups):
        first[d - 1].wait_recv()
        over[d].start()
        near[d].start()
        prefetch(1)
    for d in range(groups):
        over[d].wait_recv()
        on[d].start()
        prefetch(3)
        if d > 0:
            norm(d - 1)
    prefetch(len(ahead))
    norm(groups - 1)
    for c in told:
        c.wait_recv()

    def column(which, e):
        table = info[:, which].reshape(total, lanes)
        here = lax.broadcasted_iota(jnp.int32, (total, lanes), 1) == z * experts + e
        return jnp.sum(jnp.where(here, table, 0.0), axis=1, keepdims=True)

    def place(e, side):
        at = lax.broadcasted_iota(jnp.int32, (total, 2 * half), 1).astype(jnp.float32)
        return jnp.where(column(0, e) + float(side * half) == at, 1.0, 0.0).astype(jnp.bfloat16)

    def part_of_hidden(p):
        return hid.at[p, pl.ds(pl.multiple_of(t * units, units), units)]

    def tell(p):
        return [
            send(part_of_hidden(p), part_of_hidden(p), hid_send.at[p, i], hid_recv.at[p, i], tensor=peer)
            for i, peer in enumerate((mate, across, diagonal))
        ]

    @pl.loop(0, pairs)
    def _(p):
        slot = p % deep_gu
        for c in weights(p, slot):
            c.wait()
        acts = lax.dot_general(
            gu[slot].reshape(4 * units, shards * width), xn[...], NT, preferred_element_type=jnp.float32
        )

        @pl.when(p + deep_gu < pairs)
        def _():
            for c in weights(p + deep_gu, slot):
                c.start()

        both = jnp.zeros((units, 2 * half), jnp.float32)
        for side in range(2):
            gate = acts[2 * side * units : (2 * side + 1) * units]
            up = acts[(2 * side + 1) * units : (2 * side + 2) * units]
            hidden = (gate / (1.0 + jnp.exp(-gate)) * up).astype(jnp.bfloat16)
            both += jnp.dot(hidden, place(2 * p + side, side), preferred_element_type=jnp.float32)
        hid[p, pl.ds(pl.multiple_of(t * units, units), units), :] = both.astype(jnp.bfloat16)
        for c in tell(p):
            c.start()

    def shares(h):
        return [
            send(
                parts.at[h, (z + d) % groups], back.at[h, d], part_send.at[h, d], part_recv.at[h, d],
                expert=(z + d) % groups,
            )
            for d in range(1, groups)
        ]

    for h in range(2):
        acc[h] = jnp.zeros_like(acc[h])

        @pl.loop(0, pairs)
        def _(p):
            if h == 0:
                for c in tell(p):
                    c.wait()
                for side in range(2):
                    e = 2 * p + side
                    rows_of = lax.dot_general(place(e, side), hid[p], NT, preferred_element_type=jnp.float32)
                    spread[p, :, side * depth : (side + 1) * depth] = (rows_of * column(1, e)).astype(jnp.bfloat16)
            unit = h * pairs + p
            slot = unit % deep_dn
            for c in downs(unit, slot):
                c.wait()
            acc[h] += lax.dot_general(spread[p], dn[slot], NT, preferred_element_type=jnp.float32)

            @pl.when(unit + deep_dn < 2 * pairs)
            def _():
                for c in downs(unit + deep_dn, slot):
                    c.start()

        for b in range(groups):
            parts[h, b] = acc[h, b * rows : (b + 1) * rows, :].astype(jnp.bfloat16)
        for c in shares(h):
            c.start()

    for h in range(2):
        result = acc[h, pl.ds(pl.multiple_of(z * rows, rows), rows), :]
        for d, c in enumerate(shares(h), 1):
            c.wait_recv()
            result += back[h, d].astype(jnp.float32)
        out_ref[:, h * part : (h + 1) * part] = result.astype(jnp.bfloat16)
    for c in first + over + near + on + told + shares(0) + shares(1):
        c.wait_send()


def kernel_form(tokens, norm_gain, expert_ids, gate_weights, gate_proj, up_proj, down_proj):
    groups, shards = lax.axis_size("expert"), lax.axis_size("tensor")
    rows, width = tokens.shape
    experts, units, features = gate_proj.shape
    out_width = down_proj.shape[1]
    total, pairs, lanes = groups * rows, experts // 2, -(-EXPERTS // 128) * 128
    deep_gu, deep_dn, part = min(pairs, 4), min(2 * pairs, 8), out_width // 2
    vmem, hbm = pl.BlockSpec(memory_space=pltpu.VMEM), pl.BlockSpec(memory_space=pl.ANY)
    dma = pltpu.SemaphoreType.DMA
    flops = 2 * total * experts * (2 * units * features + out_width * down_proj.shape[2])
    return pl.pallas_call(
        kernel,
        out_shape=jax.ShapeDtypeStruct((rows, out_width), jnp.bfloat16),
        in_specs=[vmem] * 4 + [hbm] * 3,
        out_specs=vmem,
        scratch_shapes=[
            pltpu.VMEM((shards, total, width), jnp.bfloat16),
            pltpu.VMEM((total, shards * width), jnp.bfloat16),
            pltpu.VMEM((groups, 2, rows, lanes), jnp.float32),
            pltpu.VMEM((deep_gu, 2, 2, units, features), jnp.bfloat16),
            pltpu.VMEM((deep_dn, part, 2 * down_proj.shape[2]), jnp.bfloat16),
            pltpu.VMEM((pairs, shards * units, 2 * groups * CAP), jnp.bfloat16),
            pltpu.VMEM((pairs, total, 2 * down_proj.shape[2]), jnp.bfloat16),
            pltpu.VMEM((2, total, part), jnp.float32),
            pltpu.VMEM((2, groups, rows, part), jnp.bfloat16),
            pltpu.VMEM((2, groups, rows, part), jnp.bfloat16),
            dma((deep_gu, 2, 2)),
            dma((deep_dn, 2)),
            dma((4, groups)),
            dma((4, groups)),
            dma((groups,)),
            dma((groups,)),
            dma((pairs, 3)),
            dma((pairs, 3)),
            dma((2, groups)),
            dma((2, groups)),
        ],
        compiler_params=pltpu.CompilerParams(
            collective_id=0, has_side_effects=True, vmem_limit_bytes=58 * 2**20
        ),
        cost_estimate=pl.CostEstimate(flops=flops, bytes_accessed=3 * 2 * gate_proj.size, transcendentals=0),
    )(tokens, norm_gain.reshape(shards, width), expert_ids, gate_weights, gate_proj, up_proj, down_proj)


def body(tokens, norm_gain, expert_ids, gate_weights, gate_proj, up_proj, down_proj):
    form = dispatch_form
    if tokens.shape[0] < gate_proj.shape[0] * CAP:
        form = gather_form
        if lax.axis_size("tensor") == 4 and gate_proj.shape[0] % 2 == 0:
            form = kernel_form
    return form(tokens, norm_gain, expert_ids, gate_weights, gate_proj, up_proj, down_proj)


def solution(mesh):
    return jax.shard_map(
        body,
        mesh=mesh,
        in_specs=(
            P(("group", "expert"), "tensor"),
            P(),
            P(("group", "expert"), None),
            P(("group", "expert"), None),
            P("expert", "tensor", None),
            P("expert", "tensor", None),
            P("expert", "tensor", None),
        ),
        out_specs=P(("group", "expert"), "tensor"),
        check_vma=False,
    )
```
